32 devices in a mesh: blk: 8 (over z, y), par: 4 (over x, core).
Axes of the slice: x: 2, y: 2, z: 4, core: 2. Of those that a mesh axis runs over, the one named last changes fastest.
Arguments:
- log_derivs: float32 [2048, 4096], P('blk', 'par'), may hold values from -0.09375 to 0.09375
- energies: float32 [2048], P('blk'), may hold values from -6 to 6
Outputs:
- panel_tiles: float32 [2048, 256], P('blk')
- energies_next: float32 [2048], P('blk')
- diagonal_next: float32 [2048, 256], P(('blk', 'par'))
- neighbour_next: float32 [2048, 256], P(('blk', 'par'))
The draws below stay inside these ranges and needn't reach their ends.
All inputs are finite; a program needn't handle non-finite values.
Results may differ from the reference program's by a relative error of at most 0.00011.
Values sent between devices are 32-bit elements; how exact they have to be, the bound alone decides.
A program may use at most 64 MiB of HBM per device.

```python
import jax
import jax.numpy as jnp
from jax import lax

P_SIZE = 4096
B = 256
NS = 2048


def levels(own_key, extent, pieces, low, high):
    loudness = 1.0
    for position, blocks in pieces:
        heights = jax.random.uniform(jax.random.fold_in(jax.random.fold_in(own_key, 6), position), (blocks,), jnp.float32, low / len(pieces), high / len(pieces))
        loudness = loudness * jnp.repeat(jnp.exp(heights), extent[position] // blocks).reshape((-1,) + (1,) * (len(extent) - 1 - position))
    return loudness


def bell_draw(own_key, dims, width, reach, split=(), held_as=jnp.bfloat16):
    gain = levels(own_key, dims, split, -0.22, 0.18) if split else 1.0
    drawn = jax.random.normal(own_key, dims, jnp.float32) * width * gain
    return jnp.minimum(jnp.maximum(drawn, -reach), reach).astype(held_as)


def setup_inputs(seed: int = 0) -> dict:
    seeds = jax.random.split(jax.random.key(seed), 3)
    return {
        "log_derivs": bell_draw(seeds[0], (NS, P_SIZE), P_SIZE ** -0.5, 0.09375, ((0, 8), (1, 4)), jnp.float32),
        "energies": bell_draw(seeds[1], (NS,), 1.0, 6.0, ((0, 8),), jnp.float32),
    }


ridge_shift = 0.05

def kernel_tile(left_rows, right_rows):
    return jnp.dot(left_rows.astype(jnp.float32), right_rows.T.astype(jnp.float32), precision=lax.Precision.HIGHEST, preferred_element_type=jnp.float32)

def reference(log_derivs, energies):
    block_count = NS // B
    sample_blocks = log_derivs.reshape(block_count, B, P_SIZE)
    lead_rows = sample_blocks[0]
    unit_rows = jnp.eye(B, dtype=jnp.float32)
    pivot_factor = jnp.linalg.cholesky(kernel_tile(lead_rows, lead_rows) + ridge_shift * unit_rows)

    def panel_of(block_rows):
        cross_tile = kernel_tile(block_rows, lead_rows)
        return lax.linalg.triangular_solve(pivot_factor, cross_tile, left_side=False, lower=True, transpose_a=True)
    previous_blocks = jnp.roll(sample_blocks, 1, axis=0)

    def per_block(block_pair):
        block_rows, prev_block = block_pair
        panel_here = panel_of(block_rows)
        panel_prev = panel_of(prev_block)
        diag_tile = kernel_tile(block_rows, block_rows) + ridge_shift * unit_rows - kernel_tile(panel_here, panel_here)
        cycle_tile = kernel_tile(block_rows, prev_block) - kernel_tile(panel_here, panel_prev)
        return (panel_here, diag_tile, cycle_tile)
    panels, diagonals, neighbours = lax.map(per_block, (sample_blocks, previous_blocks))
    panel_tiles = panels.reshape(NS, B)
    lead_solve = lax.linalg.triangular_solve(pivot_factor, energies[:B][:, None], left_side=True, lower=True)[:, 0]
    remainder = energies - jnp.dot(panel_tiles.astype(jnp.float32), lead_solve.astype(jnp.float32), precision=lax.Precision.HIGHEST, preferred_element_type=jnp.float32)
    energies_next = jnp.concatenate([lead_solve, remainder[B:]])
    return (panel_tiles, energies_next, diagonals.reshape(NS, B), neighbours.reshape(NS, B))
```

```python
import functools

import jax
import jax.numpy as jnp
from jax import lax
from jax.experimental import pallas as pl
from jax.experimental.pallas import tpu as pltpu
from jax.sharding import PartitionSpec as P

ridge_shift = 0.05
MESH = pl.DeviceIdType.MESH
CHUNKS = 4
SELF, CROSS, PIVOT, CYCLE, BACK = range(5)


def dot_t(left, right):
    return lax.dot_general(
        left, right, (((1,), (1,)), ((), ())),
        precision=lax.Precision.HIGHEST, preferred_element_type=jnp.float32,
    )


def gather_kernel(
    nb, npar, a_ref, e_ref, full_ref, rows_ref, lead_e_ref,
    lead, prev, part, land1, land2,
    lead_send, lead_recv, e_send, e_recv, prev_send, prev_recv,
    rs_send, rs_recv, ag_send, ag_recv,
):
    b = lax.axis_index("blk")
    j = lax.axis_index("par")
    size = a_ref.shape[0]
    half = size // 2
    step = half // CHUNKS
    share = size // npar
    odd = lax.rem(b, 2)
    sib = b + 1 - 2 * odd
    nxt, prv = lax.rem(b + 1, nb), lax.rem(b + nb - 1, nb)

    def to_blk(src, dst, send, recv, target):
        return pltpu.make_async_remote_copy(
            src_ref=src, dst_ref=dst, send_sem=send, recv_sem=recv,
            device_id=(target, j), device_id_type=MESH,
        )

    def to_par(src, dst, send, recv, target):
        return pltpu.make_async_remote_copy(
            src_ref=src, dst_ref=dst, send_sem=send, recv_sem=recv,
            device_id=(b, target), device_id_type=MESH,
        )

    barrier = pltpu.get_barrier_semaphore()

    def greet(row, col):
        pl.semaphore_signal(barrier, inc=1, device_id=(row, col), device_id_type=MESH)

    greet(nxt, j)
    greet(prv, j)
    for d in range(1, npar):
        greet(b, lax.rem(j + d, npar))

    @pl.when(b + 2 < nb)
    def _():
        greet(b + 2, j)

    @pl.when(b >= 2)
    def _():
        greet(b - 2, j)

    outer = (b + 2 < nb).astype(jnp.int32) + (b >= 2).astype(jnp.int32)
    pl.semaphore_wait(barrier, 2 + npar - 1 + outer)

    def piece(h, c):
        return pl.ds(pl.multiple_of(h * half + c * step, step), step)

    def lead_copy(src_ref, h, c, kind, target):
        at = piece(h, c)
        return to_blk(
            src_ref.at[at], lead.at[at], lead_send.at[kind, c], lead_recv.at[h, c], target
        )

    main = 1 - odd

    @pl.when(b == 0)
    def _():
        for c in range(CHUNKS):
            lead_copy(a_ref, 0, c, 2, 1).start()
            if nb > 2:
                lead_copy(a_ref, 1, c, 0, 2).start()
        to_blk(e_ref, lead_e_ref, e_send.at[1], e_recv, 1).start()
        if nb > 2:
            to_blk(e_ref, lead_e_ref, e_send.at[0], e_recv, 2).start()
        for c in range(CHUNKS):
            lead_copy(a_ref, 1, c, 1, 1).start()

    prev_copy = to_blk(a_ref, prev, prev_send, prev_recv, nxt)

    @pl.when(b != 0)
    def _():
        prev_copy.start()

    part[SELF] = dot_t(a_ref[...], a_ref[...])

    @pl.when(b == 0)
    def _():
        part[CROSS] = part[SELF]
        part[PIVOT] = part[SELF]
        lead_e_ref[...] = e_ref[...]

    @pl.when(b != 0)
    def _():
        for c in range(CHUNKS):
            lead_copy(lead, main, c, 0, b).wait_recv()

            @pl.when(b + 2 < nb)
            def _():
                lead_copy(lead, main, c, 0, b + 2).start()

            @pl.when(b > 1)
            def _():
                lead_copy(lead, main, c, 1, sib).start()

        to_blk(lead_e_ref, lead_e_ref, e_send.at[0], e_recv, b).wait_recv()

        @pl.when(odd == 0)
        def _():
            to_blk(lead_e_ref, lead_e_ref, e_send.at[1], e_recv, b + 1).start()

            @pl.when(b + 2 < nb)
            def _():
                to_blk(lead_e_ref, lead_e_ref, e_send.at[0], e_recv, b + 2).start()

        for c in range(CHUNKS):
            lead_copy(lead, 1 - main, c, 0, b).wait_recv()
        part[CROSS] = dot_t(a_ref[...], lead[...])
        part[PIVOT] = dot_t(lead[...], lead[...])

    def rows_of(p):
        return pl.ds(pl.multiple_of(p * share, share), share)

    def scatter(d, phase):
        p = lax.rem(j + d, npar)
        low, high = ((SELF, PIVOT + 1), (CYCLE, BACK + 1))[phase]
        land = (land1, land2)[phase]
        return to_par(
            part.at[pl.ds(low, high - low), rows_of(p)], land.at[d - 1],
            rs_send.at[phase, d - 1], rs_recv.at[phase, d - 1], p,
        )

    def gather(d, phase):
        low, count = ((0, 2), (2, 1))[phase]
        mine = full_ref.at[pl.ds(low, count), rows_of(j)]
        return to_par(
            mine, mine, ag_send.at[phase, d - 1], ag_recv.at[phase, d - 1],
            lax.rem(j + d, npar),
        )

    def gathered(d, phase):
        low, count = ((0, 2), (2, 1))[phase]
        theirs = full_ref.at[pl.ds(low, count), rows_of(lax.rem(j + npar - d, npar))]
        return to_par(
            theirs, theirs, ag_send.at[phase, d - 1], ag_recv.at[phase, d - 1],
            lax.rem(j + d, npar),
        )

    peers = range(1, npar)
    for d in peers:
        scatter(d, 0).start()

    @pl.when(b == 1)
    def _():
        part[CYCLE] = part[CROSS]
        part[BACK] = part[PIVOT]

    @pl.when(jnp.logical_and(b != 1, b != 0))
    def _():
        prev_copy.wait_recv()
        part[CYCLE] = dot_t(a_ref[...], prev[...])
        part[BACK] = dot_t(prev[...], lead[...])

    @pl.when(b == 0)
    def _():
        prev_copy.wait_recv()
        part[CYCLE] = dot_t(a_ref[...], prev[...])
        part[BACK] = dot_t(prev[...], a_ref[...])

    for d in peers:
        scatter(d, 1).start()
    mine = rows_of(j)

    for d in peers:
        scatter(d, 0).wait_recv()

    def total(t, land, slot):
        value = part[t, mine]
        for d in peers:
            value = value + land[d - 1, slot]
        return value

    rows_ref[0] = total(SELF, land1, 0)
    full_ref[0, mine] = total(PIVOT, land1, 2)
    full_ref[1, mine] = total(CROSS, land1, 1)
    for d in peers:
        gather(d, 0).start()
    for d in peers:
        scatter(d, 1).wait_recv()
    full_ref[2, mine] = total(BACK, land2, 1)
    for d in peers:
        gather(d, 1).start()
    rows_ref[1] = total(CYCLE, land2, 0)

    for phase in range(2):
        for d in peers:
            gathered(d, phase).wait_recv()
    for phase in range(2):
        for d in peers:
            scatter(d, phase).wait_send()
            gather(d, phase).wait_send()

    @pl.when(b != 0)
    def _():
        prev_copy.wait_send()
        for c in range(CHUNKS):
            @pl.when(b + 2 < nb)
            def _():
                lead_copy(lead, main, c, 0, b + 2).wait_send()

            @pl.when(b > 1)
            def _():
                lead_copy(lead, main, c, 1, sib).wait_send()

        @pl.when(odd == 0)
        def _():
            to_blk(lead_e_ref, lead_e_ref, e_send.at[1], e_recv, b + 1).wait_send()

            @pl.when(b + 2 < nb)
            def _():
                to_blk(lead_e_ref, lead_e_ref, e_send.at[0], e_recv, b + 2).wait_send()

    @pl.when(b == 0)
    def _():
        for c in range(CHUNKS):
            lead_copy(a_ref, 0, c, 2, 1).wait_send()
            lead_copy(a_ref, 1, c, 1, 1).wait_send()
            if nb > 2:
                lead_copy(a_ref, 1, c, 0, 2).wait_send()
        to_blk(e_ref, lead_e_ref, e_send.at[1], e_recv, 1).wait_send()
        if nb > 2:
            to_blk(e_ref, lead_e_ref, e_send.at[0], e_recv, 2).wait_send()


def inverse_factor(tile):
    n = tile.shape[0]
    row_id = lax.broadcasted_iota(jnp.int32, (n, n), 0)
    col_id = lax.broadcasted_iota(jnp.int32, (n, n), 1)
    unit = (row_id == col_id).astype(jnp.float32)
    left = [tile[i * 8:(i + 1) * 8] for i in range(n // 8)]
    right = [unit[i * 8:(i + 1) * 8] for i in range(n // 8)]
    sub = lax.broadcasted_iota(jnp.int32, (8, 1), 0)
    for k in range(n):
        g, s = divmod(k, 8)
        row = left[g][s:s + 1]
        row_right = right[g][s:s + 1]
        inv = 1.0 / row[:, k:k + 1]
        row, row_right = row * inv, row_right * inv
        for i in range(g, n // 8):
            col = left[i][:, k:k + 1]
            if i == g:
                if s == 7:
                    continue
                col = jnp.where(sub > s, col, 0.0)
            left[i] = left[i] - col * row
            right[i] = right[i] - col * row_right
    left, right = jnp.concatenate(left, 0), jnp.concatenate(right, 0)
    pivots = jnp.sum(left * unit, axis=1, keepdims=True)
    return right * lax.rsqrt(pivots)


def factor_kernel(
    place_ref, full_ref, rows_ref, lead_e_ref, e_ref,
    panel_ref, e_next_ref, diag_ref, near_ref, prev_panel,
):
    size = e_ref.shape[1]
    share = rows_ref.shape[1]
    bs = size // 2
    unit = (
        lax.broadcasted_iota(jnp.int32, (bs, bs), 0) == lax.broadcasted_iota(jnp.int32, (bs, bs), 1)
    ).astype(jnp.float32) * ridge_shift
    inv0 = inverse_factor(full_ref[0, :bs, :bs] + unit)
    below = jnp.concatenate(
        [full_ref[0, bs:, :bs], full_ref[1, :, :bs], full_ref[2, :, :bs], lead_e_ref[:, :bs]], 0
    )
    rest = jnp.concatenate(
        [full_ref[0, bs:, bs:] + unit, full_ref[1, :, bs:], full_ref[2, :, bs:], lead_e_ref[:, bs:]], 0
    )
    first = dot_t(below, inv0)
    rest = rest - dot_t(first, first[:bs])
    inv1 = inverse_factor(rest[:bs])
    second = dot_t(rest[bs:], inv1)
    panel_ref[:, :bs] = first[bs:bs + size]
    panel_ref[:, bs:] = second[:size]
    prev_panel[:, :bs] = first[bs + size:bs + 2 * size]
    prev_panel[:, bs:] = second[size:2 * size]
    lead_row = jnp.concatenate([first[bs + 2 * size:], second[2 * size:]], 1)
    panel = panel_ref[...]
    remainder = e_ref[...] - dot_t(lead_row, panel)
    e_next_ref[...] = jnp.where(place_ref[0] == 0, lead_row, remainder)
    start = pl.multiple_of(place_ref[1] * share, share)
    part = panel_ref[pl.ds(start, share)]
    shift = jnp.where(
        lax.broadcasted_iota(jnp.int32, (share, size), 0) + start
        == lax.broadcasted_iota(jnp.int32, (share, size), 1),
        ridge_shift, 0.0,
    )
    diag_ref[...] = rows_ref[0] + shift - dot_t(part, panel)
    near_ref[...] = rows_ref[1] - dot_t(part, prev_panel[...])


def on_device(nb, npar, log_derivs, energies):
    size, depth = log_derivs.shape
    share = size // npar
    f32 = jnp.float32
    vmem = pl.BlockSpec(memory_space=pltpu.VMEM)
    e_rows = jnp.broadcast_to(energies[None], (8, size))
    dma = pltpu.SemaphoreType.DMA
    full, rows, lead_e = pl.pallas_call(
        functools.partial(gather_kernel, nb, npar),
        out_shape=(
            jax.ShapeDtypeStruct((3, size, size), f32),
            jax.ShapeDtypeStruct((2, share, size), f32),
            jax.ShapeDtypeStruct((8, size), f32),
        ),
        in_specs=[vmem, vmem],
        out_specs=(vmem, vmem, vmem),
        scratch_shapes=[
            pltpu.VMEM((size, depth), f32),
            pltpu.VMEM((size, depth), f32),
            pltpu.VMEM((5, size, size), f32),
            pltpu.VMEM((npar - 1, 3, share, size), f32),
            pltpu.VMEM((npar - 1, 2, share, size), f32),
            dma((3, CHUNKS)), dma((2, CHUNKS)), dma((2,)), dma, dma, dma,
            dma((2, npar - 1)), dma((2, npar - 1)), dma((2, npar - 1)), dma((2, npar - 1)),
        ],
        compiler_params=pltpu.CompilerParams(
            collective_id=0, has_side_effects=True, vmem_limit_bytes=40 * 2**20
        ),
        name="gather_tiles",
    )(log_derivs, e_rows)
    place = jnp.stack([lax.axis_index("blk"), lax.axis_index("par")]).astype(jnp.int32)
    panel, e_next, diag, near = pl.pallas_call(
        factor_kernel,
        out_shape=(
            jax.ShapeDtypeStruct((size, size), f32),
            jax.ShapeDtypeStruct((8, size), f32),
            jax.ShapeDtypeStruct((share, size), f32),
            jax.ShapeDtypeStruct((share, size), f32),
        ),
        in_specs=[pl.BlockSpec(memory_space=pltpu.SMEM), vmem, vmem, vmem, vmem],
        out_specs=(vmem, vmem, vmem, vmem),
        scratch_shapes=[pltpu.VMEM((size, size), f32)],
        compiler_params=pltpu.CompilerParams(vmem_limit_bytes=40 * 2**20),
        name="factor_tiles",
    )(place, full, rows, lead_e, e_rows)
    return panel, e_next[0], diag, near


def solution(mesh):
    nb, npar = mesh.shape["blk"], mesh.shape["par"]
    return jax.shard_map(
        functools.partial(on_device, nb, npar),
        mesh=mesh,
        in_specs=(P("blk", "par"), P("blk")),
        out_specs=(P("blk", None), P("blk"), P(("blk", "par"), None), P(("blk", "par"), None)),
        check_vma=False,
    )
```

```python
import functools

import jax
import jax.numpy as jnp
from jax import lax
from jax.experimental import pallas as pl
from jax.experimental.pallas import tpu as pltpu
from jax.sharding import PartitionSpec as P

ridge_shift = 0.05
MESH = pl.DeviceIdType.MESH
CHUNKS = 4
PREV_CHUNKS = 4
SELF, CROSS, CYCLE = range(3)
LEFT, BACK = range(2)


def dot_t(left, right):
    return lax.dot_general(
        left, right, (((1,), (1,)), ((), ())),
        precision=lax.Precision.HIGHEST, preferred_element_type=jnp.float32,
    )


def tile_kernel(
    nb, npar, a_ref, e_ref, panel_ref, e_next_ref, diag_ref, near_ref,
    lead, prev, part, land, full, fac, back_panel,
    lead_send, lead_recv, fac_send, fac_recv, share_send, share_recv,
    prev_send, prev_recv, rs_send, rs_recv, ag_send, ag_recv, back_send, back_recv,
):
    b = lax.axis_index("blk")
    j = lax.axis_index("par")
    size = a_ref.shape[0]
    half = size // 2
    step = half // CHUNKS
    share = size // npar
    bs = half
    odd = lax.rem(b, 2)
    sib = b + 1 - 2 * odd
    nxt, prv = lax.rem(b + 1, nb), lax.rem(b + nb - 1, nb)
    peers = range(1, npar)

    def to_blk(src, dst, send, recv, target):
        return pltpu.make_async_remote_copy(
            src_ref=src, dst_ref=dst, send_sem=send, recv_sem=recv,
            device_id=(target, j), device_id_type=MESH,
        )

    def to_par(src, dst, send, recv, target):
        return pltpu.make_async_remote_copy(
            src_ref=src, dst_ref=dst, send_sem=send, recv_sem=recv,
            device_id=(b, target), device_id_type=MESH,
        )

    barrier = pltpu.get_barrier_semaphore()

    def greet(row, col):
        pl.semaphore_signal(barrier, inc=1, device_id=(row, col), device_id_type=MESH)

    greet(nxt, j)
    greet(prv, j)
    for d in range(1, npar):
        greet(b, lax.rem(j + d, npar))

    @pl.when(b + 2 < nb)
    def _():
        greet(b + 2, j)

    @pl.when(b >= 2)
    def _():
        greet(b - 2, j)

    outer = (b + 2 < nb).astype(jnp.int32) + (b >= 2).astype(jnp.int32)
    pl.semaphore_wait(barrier, 2 + npar - 1 + outer)

    def piece(h, c):
        return pl.ds(pl.multiple_of(h * half + c * step, step), step)

    def lead_copy(src_ref, h, c, kind, target):
        at = piece(h, c)
        return to_blk(
            src_ref.at[at], lead.at[at], lead_send.at[kind, c], lead_recv.at[h, c], target
        )

    main = 1 - odd

    @pl.when(b == 0)
    def _():
        for c in range(CHUNKS):
            lead_copy(a_ref, 0, c, 2, 1).start()
            if nb > 2:
                lead_copy(a_ref, 1, c, 0, 2).start()
        for c in range(CHUNKS):
            lead_copy(a_ref, 1, c, 1, 1).start()

    prev_step = size // PREV_CHUNKS

    def prev_copy(q):
        at = pl.ds(q * prev_step, prev_step)
        return to_blk(a_ref.at[at], prev.at[at], prev_send.at[q], prev_recv.at[q], nxt)

    def rows_of(p, count):
        return pl.ds(pl.multiple_of(p * count, 8), count)

    mine = rows_of(j, share)

    def scatter(d, t):
        p = lax.rem(j + d, npar)
        return to_par(
            part.at[t, rows_of(p, share)], land.at[t, d - 1],
            rs_send.at[t, d - 1], rs_recv.at[t, d - 1], p,
        )

    def total(t):
        value = part[t, mine]
        for d in peers:
            scatter(d, t).wait_recv()
            value = value + land[t, d - 1]
        return value

    def gather(d, t, owner):
        at = full.at[t, rows_of(owner, share)]
        return to_par(at, at, ag_send.at[t, d - 1], ag_recv.at[t, d - 1], lax.rem(j + d, npar))

    def wait_gathered(t):
        for d in peers:
            gather(d, t, lax.rem(j + npar - d, npar)).wait_recv()

    fac_share = fac.shape[0] // npar

    def pass_fac(kind, target):
        at = fac.at[rows_of(j, fac_share)]
        return to_blk(at, at, fac_send.at[kind], fac_recv, target)

    def share_fac(d, owner):
        at = fac.at[rows_of(owner, fac_share)]
        return to_par(at, at, share_send.at[d - 1], share_recv.at[d - 1], lax.rem(j + d, npar))

    def back_copy():
        return to_blk(full.at[LEFT, mine], full.at[BACK, mine], back_send, back_recv, nxt)

    @pl.when(b != 0)
    def _():
        for q in range(PREV_CHUNKS // 2):
            prev_copy(q).start()

    part[SELF] = dot_t(a_ref[...], a_ref[...])

    @pl.when(b == 0)
    def _():
        part[CROSS] = part[SELF]

    @pl.when(b != 0)
    def _():
        for d in peers:
            scatter(d, SELF).start()
        for c in range(CHUNKS):
            lead_copy(lead, main, c, 0, b).wait_recv()

            @pl.when(b + 2 < nb)
            def _():
                lead_copy(lead, main, c, 0, b + 2).start()

            @pl.when(b > 1)
            def _():
                lead_copy(lead, main, c, 1, sib).start()

            if c % 2 == 1:
                prev_copy(PREV_CHUNKS // 2 + c // 2).start()
        for c in range(CHUNKS):
            lead_copy(lead, 1 - main, c, 0, b).wait_recv()
        part[CROSS] = dot_t(a_ref[...], lead[...])

    for d in peers:
        scatter(d, CROSS).start()

    @pl.when(b == 0)
    def _():
        for d in peers:
            scatter(d, SELF).start()

    full[LEFT, mine] = total(CROSS)
    for d in peers:
        gather(d, LEFT, j).start()
    back_copy().start()

    @pl.when(b == 0)
    def _():
        wait_gathered(LEFT)
        unit = (
            lax.broadcasted_iota(jnp.int32, (bs, bs), 0)
            == lax.broadcasted_iota(jnp.int32, (bs, bs), 1)
        ).astype(jnp.float32) * ridge_shift
        inv0 = inverse_factor(full[LEFT, :bs, :bs] + unit)
        low = dot_t(full[LEFT, bs:, :bs], inv0)
        inv1 = inverse_factor(full[LEFT, bs:, bs:] + unit - dot_t(low, low))
        lead0 = dot_t(e_ref[:, :bs], inv0)
        lead1 = dot_t(e_ref[:, bs:] - dot_t(lead0, low), inv1)
        fac[0:bs] = inv0
        fac[bs:2 * bs] = low
        fac[2 * bs:3 * bs] = inv1
        fac[3 * bs:3 * bs + 8] = lead0
        fac[3 * bs + 8:3 * bs + 16] = lead1
        fac[3 * bs + 16:] = jnp.zeros((fac.shape[0] - 3 * bs - 16, bs), jnp.float32)
        pass_fac(1, 1).start()
        if nb > 2:
            pass_fac(0, 2).start()

    @pl.when(b != 0)
    def _():
        pass_fac(0, b).wait_recv()

        @pl.when(odd == 0)
        def _():
            pass_fac(1, b + 1).start()

            @pl.when(b + 2 < nb)
            def _():
                pass_fac(0, b + 2).start()

        for d in peers:
            share_fac(d, j).start()

    diag = total(SELF)
    back_copy().wait_recv()
    for d in peers:
        gather(d, BACK, j).start()

    @pl.when(b == 1)
    def _():
        part[CYCLE] = part[CROSS]

    @pl.when(b != 1)
    def _():
        for q in range(PREV_CHUNKS):
            prev_copy(q).wait_recv()
        part[CYCLE] = dot_t(a_ref[...], prev[...])

    for d in peers:
        scatter(d, CYCLE).start()

    @pl.when(b != 0)
    def _():
        wait_gathered(LEFT)
        for d in peers:
            share_fac(d, lax.rem(j + npar - d, npar)).wait_recv()

    def solve(t, out):
        first = dot_t(full[t, :, :bs], fac[0:bs])
        second = full[t, :, bs:] - dot_t(first, fac[bs:2 * bs])
        out[:, :bs] = first
        out[:, bs:] = dot_t(second, fac[2 * bs:3 * bs])

    solve(LEFT, panel_ref)
    lead_row = jnp.concatenate([fac[3 * bs:3 * bs + 8], fac[3 * bs + 8:3 * bs + 16]], 1)
    panel = panel_ref[...]
    remainder = e_ref[...] - dot_t(lead_row, panel)
    e_next_ref[...] = jnp.where(b == 0, lead_row, remainder)
    panel_rows = panel_ref[mine]
    shift = jnp.where(
        lax.broadcasted_iota(jnp.int32, (share, size), 0) + j * share
        == lax.broadcasted_iota(jnp.int32, (share, size), 1),
        ridge_shift, 0.0,
    )
    diag_ref[...] = diag + shift - dot_t(panel_rows, panel)
    wait_gathered(BACK)
    solve(BACK, back_panel)
    taken = dot_t(panel_rows, back_panel[...])
    near_ref[...] = total(CYCLE) - taken

    for d in peers:
        for t in (SELF, CROSS, CYCLE):
            scatter(d, t).wait_send()
        for t in (LEFT, BACK):
            gather(d, t, j).wait_send()
    back_copy().wait_send()

    @pl.when(b != 0)
    def _():
        for q in range(PREV_CHUNKS):
            prev_copy(q).wait_send()
        for d in peers:
            share_fac(d, j).wait_send()
        for c in range(CHUNKS):
            @pl.when(b + 2 < nb)
            def _():
                lead_copy(lead, main, c, 0, b + 2).wait_send()

            @pl.when(b > 1)
            def _():
                lead_copy(lead, main, c, 1, sib).wait_send()

        @pl.when(odd == 0)
        def _():
            pass_fac(1, b + 1).wait_send()

            @pl.when(b + 2 < nb)
            def _():
                pass_fac(0, b + 2).wait_send()

    @pl.when(b == 0)
    def _():
        for c in range(CHUNKS):
            lead_copy(a_ref, 0, c, 2, 1).wait_send()
            lead_copy(a_ref, 1, c, 1, 1).wait_send()
            if nb > 2:
                lead_copy(a_ref, 1, c, 0, 2).wait_send()
        pass_fac(1, 1).wait_send()
        if nb > 2:
            pass_fac(0, 2).wait_send()


def inverse_factor(tile):
    n = tile.shape[0]
    row_id = lax.broadcasted_iota(jnp.int32, (n, n), 0)
    col_id = lax.broadcasted_iota(jnp.int32, (n, n), 1)
    unit = (row_id == col_id).astype(jnp.float32)
    left = [tile[i * 8:(i + 1) * 8] for i in range(n // 8)]
    right = [unit[i * 8:(i + 1) * 8] for i in range(n // 8)]
    sub = lax.broadcasted_iota(jnp.int32, (8, 1), 0)
    for k in range(n):
        g, s = divmod(k, 8)
        row = left[g][s:s + 1]
        row_right = right[g][s:s + 1]
        inv = 1.0 / row[:, k:k + 1]
        row, row_right = row * inv, row_right * inv
        for i in range(g, n // 8):
            col = left[i][:, k:k + 1]
            if i == g:
                if s == 7:
                    continue
                col = jnp.where(sub > s, col, 0.0)
            left[i] = left[i] - col * row
            right[i] = right[i] - col * row_right
    left, right = jnp.concatenate(left, 0), jnp.concatenate(right, 0)
    pivots = jnp.sum(left * unit, axis=1, keepdims=True)
    return right * lax.rsqrt(pivots)


def on_device(nb, npar, log_derivs, energies):
    size, depth = log_derivs.shape
    share = size // npar
    fac_rows = ((3 * (size // 2) + 16) // (8 * npar) + 1) * 8 * npar
    f32 = jnp.float32
    vmem = pl.BlockSpec(memory_space=pltpu.VMEM)
    e_rows = jnp.broadcast_to(energies[None], (8, size))
    dma = pltpu.SemaphoreType.DMA
    panel, e_next, diag, near = pl.pallas_call(
        functools.partial(tile_kernel, nb, npar),
        out_shape=(
            jax.ShapeDtypeStruct((size, size), f32),
            jax.ShapeDtypeStruct((8, size), f32),
            jax.ShapeDtypeStruct((share, size), f32),
            jax.ShapeDtypeStruct((share, size), f32),
        ),
        in_specs=[vmem, vmem],
        out_specs=(vmem, vmem, vmem, vmem),
        scratch_shapes=[
            pltpu.VMEM((size, depth), f32),
            pltpu.VMEM((size, depth), f32),
            pltpu.VMEM((3, size, size), f32),
            pltpu.VMEM((3, npar - 1, share, size), f32),
            pltpu.VMEM((2, size, size), f32),
            pltpu.VMEM((fac_rows, size // 2), f32),
            pltpu.VMEM((size, size), f32),
            dma((3, CHUNKS)), dma((2, CHUNKS)), dma((2,)), dma,
            dma((npar - 1,)), dma((npar - 1,)), dma((PREV_CHUNKS,)), dma((PREV_CHUNKS,)),
            dma((3, npar - 1)), dma((3, npar - 1)), dma((2, npar - 1)), dma((2, npar - 1)),
            dma, dma,
        ],
        compiler_params=pltpu.CompilerParams(
            collective_id=0, has_side_effects=True, vmem_limit_bytes=40 * 2**20
        ),
        name="all_tiles",
    )(log_derivs, e_rows)
    return panel, e_next[0], diag, near


def solution(mesh):
    nb, npar = mesh.shape["blk"], mesh.shape["par"]
    return jax.shard_map(
        functools.partial(on_device, nb, npar),
        mesh=mesh,
        in_specs=(P("blk", "par"), P("blk")),
        out_specs=(P("blk", None), P("blk"), P(("blk", "par"), None), P(("blk", "par"), None)),
        check_vma=False,
    )
```

```python
import functools

import jax
import jax.numpy as jnp
from jax import lax
from jax.experimental import pallas as pl
from jax.experimental.pallas import tpu as pltpu
from jax.sharding import PartitionSpec as P

ridge_shift = 0.05
MESH = pl.DeviceIdType.MESH
CHUNKS = 16
PREV_CHUNKS = 8
PREV_EARLY = 4
SELF, CROSS, CYCLE = range(3)
LEFT, BACK = range(2)


def dot_t(left, right):
    return lax.dot_general(
        left, right, (((1,), (1,)), ((), ())),
        precision=lax.Precision.HIGHEST, preferred_element_type=jnp.float32,
    )


def tile_kernel(
    nb, npar, a_ref, e_ref, panel_ref, e_next_ref, diag_ref, near_ref,
    lead, prev, part, land, full, fac, back_panel,
    lead_send, lead_recv, fac_send, fac_recv, share_send, share_recv,
    prev_send, prev_recv, rs_send, rs_recv, ag_send, ag_recv, back_send, back_recv,
):
    b = lax.axis_index("blk")
    j = lax.axis_index("par")
    size = a_ref.shape[0]
    half = size // 2
    step = half // CHUNKS
    share = size // npar
    bs = half
    odd = lax.rem(b, 2)
    sib = b + 1 - 2 * odd
    nxt, prv = lax.rem(b + 1, nb), lax.rem(b + nb - 1, nb)
    peers = range(1, npar)

    def to_blk(src, dst, send, recv, target):
        return pltpu.make_async_remote_copy(
            src_ref=src, dst_ref=dst, send_sem=send, recv_sem=recv,
            device_id=(target, j), device_id_type=MESH,
        )

    def to_par(src, dst, send, recv, target):
        return pltpu.make_async_remote_copy(
            src_ref=src, dst_ref=dst, send_sem=send, recv_sem=recv,
            device_id=(b, target), device_id_type=MESH,
        )

    barrier = pltpu.get_barrier_semaphore()

    def greet(row, col):
        pl.semaphore_signal(barrier, inc=1, device_id=(row, col), device_id_type=MESH)

    greet(nxt, j)
    greet(prv, j)
    for d in range(1, npar):
        greet(b, lax.rem(j + d, npar))

    @pl.when(b + 2 < nb)
    def _():
        greet(b + 2, j)

    @pl.when(b >= 2)
    def _():
        greet(b - 2, j)

    outer = (b + 2 < nb).astype(jnp.int32) + (b >= 2).astype(jnp.int32)
    pl.semaphore_wait(barrier, 2 + npar - 1 + outer)

    def piece(h, c):
        return pl.ds(pl.multiple_of(h * half + c * step, step), step)

    def lead_copy(src_ref, h, c, kind, target):
        at = piece(h, c)
        return to_blk(
            src_ref.at[at], lead.at[at], lead_send.at[kind, c], lead_recv.at[h, c], target
        )

    main = 1 - odd

    @pl.when(b == 0)
    def _():
        for c in range(CHUNKS):
            lead_copy(a_ref, 0, c, 2, 1).start()
            if nb > 2:
                lead_copy(a_ref, 1, c, 0, 2).start()
        if nb <= 2:
            for c in range(CHUNKS):
                lead_copy(a_ref, 1, c, 1, 1).start()

    prev_step = size // PREV_CHUNKS

    def prev_copy(q):
        at = pl.ds(q * prev_step, prev_step)
        return to_blk(a_ref.at[at], prev.at[at], prev_send.at[q], prev_recv.at[q], nxt)

    def rows_of(p, count):
        return pl.ds(pl.multiple_of(p * count, 8), count)

    mine = rows_of(j, share)

    def scatter(d, t):
        p = lax.rem(j + d, npar)
        return to_par(
            part.at[t, rows_of(p, share)], land.at[t, d - 1],
            rs_send.at[t, d - 1], rs_recv.at[t, d - 1], p,
        )

    def total(t):
        value = part[t, mine]
        for d in peers:
            scatter(d, t).wait_recv()
            value = value + land[t, d - 1]
        return value

    def gather(d, t, owner):
        at = full.at[t, rows_of(owner, share)]
        return to_par(at, at, ag_send.at[t, d - 1], ag_recv.at[t, d - 1], lax.rem(j + d, npar))

    def wait_gathered(t):
        for d in peers:
            gather(d, t, lax.rem(j + npar - d, npar)).wait_recv()

    fac_share = fac.shape[0] // npar

    def pass_fac(kind, target):
        at = fac.at[rows_of(j, fac_share)]
        return to_blk(at, at, fac_send.at[kind], fac_recv, target)

    def share_fac(d, owner):
        at = fac.at[rows_of(owner, fac_share)]
        return to_par(at, at, share_send.at[d - 1], share_recv.at[d - 1], lax.rem(j + d, npar))

    def back_copy():
        return to_blk(full.at[LEFT, mine], full.at[BACK, mine], back_send, back_recv, nxt)

    @pl.when(b != 0)
    def _():
        for q in range(PREV_EARLY):
            prev_copy(q).start()

    part[SELF] = dot_t(a_ref[...], a_ref[...])

    @pl.when(b == 0)
    def _():
        part[CROSS] = part[SELF]

    @pl.when(b != 0)
    def _():
        for d in peers:
            scatter(d, SELF).start()
        for c in range(CHUNKS):
            lead_copy(lead, main, c, 0, b).wait_recv()

            @pl.when(b + 2 < nb)
            def _():
                lead_copy(lead, main, c, 0, b + 2).start()

            @pl.when(b > 1)
            def _():
                lead_copy(lead, main, c, 1, sib).start()

            @pl.when(b == 3)
            def _():
                lead_copy(lead, 1, c, 0, b).wait_recv()
                lead_copy(lead, 1, c, 2, 1).start()

            late = PREV_CHUNKS - PREV_EARLY
            for q in range(late):
                if c == (q + 1) * CHUNKS // late - 1:
                    prev_copy(PREV_EARLY + q).start()

        @pl.when(b != 3)
        def _():
            for c in range(CHUNKS):
                lead_copy(lead, 1 - main, c, 0, b).wait_recv()

        part[CROSS] = dot_t(a_ref[...], lead[...])

    for d in peers:
        scatter(d, CROSS).start()

    @pl.when(b == 0)
    def _():
        for d in peers:
            scatter(d, SELF).start()

    full[LEFT, mine] = total(CROSS)
    for d in peers:
        gather(d, LEFT, j).start()
    back_copy().start()

    @pl.when(b == 0)
    def _():
        wait_gathered(LEFT)
        unit = (
            lax.broadcasted_iota(jnp.int32, (bs, bs), 0)
            == lax.broadcasted_iota(jnp.int32, (bs, bs), 1)
        ).astype(jnp.float32) * ridge_shift
        inv0 = inverse_factor(full[LEFT, :bs, :bs] + unit)
        low = dot_t(full[LEFT, bs:, :bs], inv0)
        inv1 = inverse_factor(full[LEFT, bs:, bs:] + unit - dot_t(low, low))
        lead0 = dot_t(e_ref[:, :bs], inv0)
        lead1 = dot_t(e_ref[:, bs:] - dot_t(lead0, low), inv1)
        fac[0:bs] = inv0
        fac[bs:2 * bs] = low
        fac[2 * bs:3 * bs] = inv1
        fac[3 * bs:3 * bs + 8] = lead0
        fac[3 * bs + 8:3 * bs + 16] = lead1
        fac[3 * bs + 16:] = jnp.zeros((fac.shape[0] - 3 * bs - 16, bs), jnp.float32)
        pass_fac(1, 1).start()
        if nb > 2:
            pass_fac(0, 2).start()

    @pl.when(b != 0)
    def _():
        pass_fac(0, b).wait_recv()

        @pl.when(odd == 0)
        def _():
            pass_fac(1, b + 1).start()

            @pl.when(b + 2 < nb)
            def _():
                pass_fac(0, b + 2).start()

        for d in peers:
            share_fac(d, j).start()

    diag = total(SELF)
    back_copy().wait_recv()
    for d in peers:
        gather(d, BACK, j).start()

    @pl.when(b == 1)
    def _():
        part[CYCLE] = part[CROSS]

    @pl.when(b != 1)
    def _():
        for q in range(PREV_CHUNKS):
            prev_copy(q).wait_recv()
        part[CYCLE] = dot_t(a_ref[...], prev[...])

    for d in peers:
        scatter(d, CYCLE).start()

    @pl.when(b != 0)
    def _():
        wait_gathered(LEFT)
        for d in peers:
            share_fac(d, lax.rem(j + npar - d, npar)).wait_recv()

    def solve(t, out):
        first = dot_t(full[t, :, :bs], fac[0:bs])
        second = full[t, :, bs:] - dot_t(first, fac[bs:2 * bs])
        out[:, :bs] = first
        out[:, bs:] = dot_t(second, fac[2 * bs:3 * bs])

    solve(LEFT, panel_ref)
    lead_row = jnp.concatenate([fac[3 * bs:3 * bs + 8], fac[3 * bs + 8:3 * bs + 16]], 1)
    panel = panel_ref[...]
    remainder = e_ref[...] - dot_t(lead_row, panel)
    e_next_ref[...] = jnp.where(b == 0, lead_row, remainder)
    panel_rows = panel_ref[mine]
    shift = jnp.where(
        lax.broadcasted_iota(jnp.int32, (share, size), 0) + j * share
        == lax.broadcasted_iota(jnp.int32, (share, size), 1),
        ridge_shift, 0.0,
    )
    diag_ref[...] = diag + shift - dot_t(panel_rows, panel)
    wait_gathered(BACK)
    solve(BACK, back_panel)
    taken = dot_t(panel_rows, back_panel[...])
    near_ref[...] = total(CYCLE) - taken

    for d in peers:
        for t in (SELF, CROSS, CYCLE):
            scatter(d, t).wait_send()
        for t in (LEFT, BACK):
            gather(d, t, j).wait_send()
    back_copy().wait_send()

    @pl.when(b != 0)
    def _():
        for q in range(PREV_CHUNKS):
            prev_copy(q).wait_send()
        for d in peers:
            share_fac(d, j).wait_send()
        for c in range(CHUNKS):
            @pl.when(b + 2 < nb)
            def _():
                lead_copy(lead, main, c, 0, b + 2).wait_send()

            @pl.when(b > 1)
            def _():
                lead_copy(lead, main, c, 1, sib).wait_send()

            @pl.when(b == 3)
            def _():
                lead_copy(lead, 1, c, 2, 1).wait_send()

        @pl.when(odd == 0)
        def _():
            pass_fac(1, b + 1).wait_send()

            @pl.when(b + 2 < nb)
            def _():
                pass_fac(0, b + 2).wait_send()

    @pl.when(b == 0)
    def _():
        for c in range(CHUNKS):
            lead_copy(a_ref, 0, c, 2, 1).wait_send()
            lead_copy(a_ref, 1, c, int(nb > 2) ^ 1, 2 if nb > 2 else 1).wait_send()
        pass_fac(1, 1).wait_send()
        if nb > 2:
            pass_fac(0, 2).wait_send()


def inverse_factor(tile):
    n = tile.shape[0]
    row_id = lax.broadcasted_iota(jnp.int32, (n, n), 0)
    col_id = lax.broadcasted_iota(jnp.int32, (n, n), 1)
    unit = (row_id == col_id).astype(jnp.float32)
    left = [tile[i * 8:(i + 1) * 8] for i in range(n // 8)]
    right = [unit[i * 8:(i + 1) * 8] for i in range(n // 8)]
    sub = lax.broadcasted_iota(jnp.int32, (8, 1), 0)
    for k in range(n):
        g, s = divmod(k, 8)
        row = left[g][s:s + 1]
        row_right = right[g][s:s + 1]
        inv = 1.0 / row[:, k:k + 1]
        row, row_right = row * inv, row_right * inv
        for i in range(g, n // 8):
            col = left[i][:, k:k + 1]
            if i == g:
                if s == 7:
                    continue
                col = jnp.where(sub > s, col, 0.0)
            left[i] = left[i] - col * row
            right[i] = right[i] - col * row_right
    left, right = jnp.concatenate(left, 0), jnp.concatenate(right, 0)
    pivots = jnp.sum(left * unit, axis=1, keepdims=True)
    return right * lax.rsqrt(pivots)


def on_device(nb, npar, log_derivs, energies):
    size, depth = log_derivs.shape
    share = size // npar
    fac_rows = ((3 * (size // 2) + 16) // (8 * npar) + 1) * 8 * npar
    f32 = jnp.float32
    vmem = pl.BlockSpec(memory_space=pltpu.VMEM)
    e_rows = jnp.broadcast_to(energies[None], (8, size))
    dma = pltpu.SemaphoreType.DMA
    panel, e_next, diag, near = pl.pallas_call(
        functools.partial(tile_kernel, nb, npar),
        out_shape=(
            jax.ShapeDtypeStruct((size, size), f32),
            jax.ShapeDtypeStruct((8, size), f32),
            jax.ShapeDtypeStruct((share, size), f32),
            jax.ShapeDtypeStruct((share, size), f32),
        ),
        in_specs=[vmem, vmem],
        out_specs=(vmem, vmem, vmem, vmem),
        scratch_shapes=[
            pltpu.VMEM((size, depth), f32),
            pltpu.VMEM((size, depth), f32),
            pltpu.VMEM((3, size, size), f32),
            pltpu.VMEM((3, npar - 1, share, size), f32),
            pltpu.VMEM((2, size, size), f32),
            pltpu.VMEM((fac_rows, size // 2), f32),
            pltpu.VMEM((size, size), f32),
            dma((3, CHUNKS)), dma((2, CHUNKS)), dma((2,)), dma,
            dma((npar - 1,)), dma((npar - 1,)), dma((PREV_CHUNKS,)), dma((PREV_CHUNKS,)),
            dma((3, npar - 1)), dma((3, npar - 1)), dma((2, npar - 1)), dma((2, npar - 1)),
            dma, dma,
        ],
        compiler_params=pltpu.CompilerParams(
            collective_id=0, has_side_effects=True, vmem_limit_bytes=40 * 2**20
        ),
        name="all_tiles",
    )(log_derivs, e_rows)
    return panel, e_next[0], diag, near


def solution(mesh):
    nb, npar = mesh.shape["blk"], mesh.shape["par"]
    return jax.shard_map(
        functools.partial(on_device, nb, npar),
        mesh=mesh,
        in_specs=(P("blk", "par"), P("blk")),
        out_specs=(P("blk", None), P("blk"), P(("blk", "par"), None), P(("blk", "par"), None)),
        check_vma=False,
    )
```
